32 devices in a mesh: batch: 4 (over y, x), ctx: 8 (over z, core).
Axes of the slice: x: 2, y: 2, z: 4, core: 2. Of those that a mesh axis runs over, the one named last changes fastest.
Arguments:
- inputs: bfloat16 [8, 1024, 768], P('batch', 'ctx'), may hold values from -6 to 6
- cotangent: bfloat16 [8, 1024, 768], P('batch', 'ctx'), may hold values from -6 to 6
- lengths: int32 [8, 4], P('batch'), may hold values from 1 to 640, 1024 in all within a row
- qkv_weight: float32 [2304, 768], P(('batch', 'ctx')), may hold values from -0.3125 to 0.3125
- qkv_moment: float32 [2304, 768], P(('batch', 'ctx')), may hold values from -32 to 32
- qkv_square: float32 [2304, 768], P(('batch', 'ctx')), may hold values from 106.496 to 434.176
- out_weight: float32 [768, 768], P(('batch', 'ctx')), may hold values from -0.3125 to 0.3125
- out_moment: float32 [768, 768], P(('batch', 'ctx')), may hold values from -20 to 20
- out_square: float32 [768, 768], P(('batch', 'ctx')), may hold values from 81.92 to 409.6
- fc_weight: float32 [3072, 768], P(('batch', 'ctx')), may hold values from -0.21875 to 0.21875
- fc_moment: float32 [3072, 768], P(('batch', 'ctx')), may hold values from -16 to 16
- fc_square: float32 [3072, 768], P(('batch', 'ctx')), may hold values from 38.5024 to 155.648
- proj_weight: float32 [3072, 768], P(('batch', 'ctx')), may hold values from -0.109375 to 0.109375
- proj_moment: float32 [3072, 768], P(('batch', 'ctx')), may hold values from -32 to 32
- proj_square: float32 [3072, 768], P(('batch', 'ctx')), may hold values from 155.648 to 622.592
- vectors: float32 [12, 768], P(None, ('batch', 'ctx')), may hold values from -1.2 to 2.2
- vectors_moment: float32 [12, 768], P(None, ('batch', 'ctx')), may hold values from -64 to 64
- vectors_square: float32 [12, 768], P(None, ('batch', 'ctx')), may hold values from 434.176 to 1720.32
Outputs:
- layer_out: bfloat16 [8, 1024, 768], P('batch', 'ctx')
- input_grad: bfloat16 [8, 1024, 768], P('batch', 'ctx')
- qkv_grad: float32 [2304, 768], P(('batch', 'ctx'))
- qkv_moment_new: float32 [2304, 768], P(('batch', 'ctx'))
- qkv_square_new: float32 [2304, 768], P(('batch', 'ctx'))
- qkv_weight_new: float32 [2304, 768], P(('batch', 'ctx'))
- out_grad: float32 [768, 768], P(('batch', 'ctx'))
- out_moment_new: float32 [768, 768], P(('batch', 'ctx'))
- out_square_new: float32 [768, 768], P(('batch', 'ctx'))
- out_weight_new: float32 [768, 768], P(('batch', 'ctx'))
- fc_grad: float32 [3072, 768], P(('batch', 'ctx'))
- fc_moment_new: float32 [3072, 768], P(('batch', 'ctx'))
- fc_square_new: float32 [3072, 768], P(('batch', 'ctx'))
- fc_weight_new: float32 [3072, 768], P(('batch', 'ctx'))
- proj_grad: float32 [3072, 768], P(('batch', 'ctx'))
- proj_moment_new: float32 [3072, 768], P(('batch', 'ctx'))
- proj_square_new: float32 [3072, 768], P(('batch', 'ctx'))
- proj_weight_new: float32 [3072, 768], P(('batch', 'ctx'))
- vectors_grad: float32 [12, 768], P(None, ('batch', 'ctx'))
- vectors_moment_new: float32 [12, 768], P(None, ('batch', 'ctx'))
- vectors_square_new: float32 [12, 768], P(None, ('batch', 'ctx'))
- vectors_new: float32 [12, 768], P(None, ('batch', 'ctx'))
The draws below stay inside these ranges and needn't reach their ends.
Inputs may be any that keep to these rules, and one draw needn't show every extreme that they name: Each row holds 4 document lengths that sum to 1024; the longest is exactly 640.
All inputs are finite; a program needn't handle non-finite values.
Results may differ from the reference program's by a relative error of at most 0.017.
The reference program's roundings to bfloat16 on the way count: a program that leaves them out, or rounds other values in their place, can miss the bound.
Values may be sent and summed in bfloat16 or wider, within the bound.
A program may use at most 256 MiB of HBM per device.

```python
import math
import jax
import jax.numpy as jnp
import numpy as np
from jax import lax

D = 768
H = 12
HD = 64
FF = 3072
SEQ_DEV = 128
NDOC = 4
STEP = 10
LEN = 1024
SEQS = 8
TOKENS = 8192
MOST = 640
N_CTX = 8


def draw_vectors(key, part):
    key = jax.random.fold_in(key, 11)
    row_index = jnp.arange(12)[:, None]
    is_gain = ((row_index == 0) | (row_index == 5)).astype(jnp.float32)
    spread_part = 0.3 * jax.random.normal(key, (12, D), jnp.float32)
    return jnp.clip(spread_part, -1.2, 1.2) + is_gain


def block_scale(key, extent, cuts, smallest, top_value):
    gain = 1.0
    for position, shards_of in cuts:
        steps = jax.random.uniform(jax.random.fold_in(jax.random.fold_in(key, 6), position), (shards_of,), jnp.float32, smallest / len(cuts), top_value / len(cuts))
        gain = gain * jnp.repeat(jnp.exp(steps), extent[position] // shards_of).reshape((-1,) + (1,) * (len(extent) - 1 - position))
    return gain


def length_profile(amount, total, most, lean):
    portions = [(1 << 20) // math.isqrt(grade ** lean) + 1 for grade in range(2, amount + 1)]
    rest, counts = total - most - (amount - 1), [1] * (amount - 1)
    while rest > 0:
        free = [i for i in range(amount - 1) if counts[i] < most]
        mass, left = sum([portions[i] for i in free]), rest
        for i in free:
            extra = min(most - counts[i], max(1, left * portions[i] // mass), rest)
            counts[i] = counts[i] + extra
            rest = rest - extra
    return np.array([most] + counts)


def ragged(key, amount, total, most, skew):
    if amount == 2:
        one = jax.random.randint(key, (), max(1, total - most), min(most, total - 1) + 1)
        return jnp.stack([one, total - one])
    sizes = jnp.asarray(length_profile(amount, total, most, skew), jnp.int32)
    pairs = (amount - 1) // 2
    donor, sink = sizes[1:1 + 2 * pairs:2], sizes[2:2 + 2 * pairs:2]
    room = jnp.minimum(donor - 1, most - sink)
    shifted = jax.random.randint(jax.random.fold_in(key, 1), (pairs,), 0, 1 << 20) % (room + 1)
    sizes = sizes.at[1:1 + 2 * pairs:2].set(donor - shifted).at[2:2 + 2 * pairs:2].set(sink + shifted)
    return sizes[jax.random.permutation(jax.random.fold_in(key, 2), amount)]


def normal_values(own_key, shape, width, limit, split=(), held_as=jnp.bfloat16):
    level = block_scale(own_key, shape, split, -0.22, 0.18) if split else 1.0
    values = jax.random.normal(own_key, shape, jnp.float32) * width * level
    return jnp.minimum(jnp.maximum(values, -limit), limit).astype(held_as)


def setup_inputs(seed: int = 0) -> dict:
    seeds = jax.random.split(jax.random.key(seed), 19)
    return {
        "inputs": normal_values(seeds[0], (SEQS, LEN, D), 1.0, 6.0, ((0, 4), (1, 8))),
        "cotangent": normal_values(seeds[1], (SEQS, LEN, D), 1.0, 6.0, ((0, 4), (1, 8))),
        "lengths": jax.vmap(lambda own: ragged(own, NDOC, LEN, MOST, 1))(jax.random.split(seeds[2], SEQS)).reshape((SEQS, NDOC)).astype(jnp.int32),
        "qkv_weight": normal_values(seeds[3], (3 * D, D), (D // 2) ** -0.5, 0.3125, ((0, 32),), jnp.float32),
        "qkv_moment": normal_values(seeds[4], (3 * D, D), (0.055 * TOKENS ** 0.5), 32.0, ((0, 32),), jnp.float32),
        "qkv_square": jnp.clip(jnp.exp(math.log(434.176) - 1.40534252 * jax.random.uniform(seeds[5], (3 * D, D), jnp.float32) ** block_scale(seeds[5], (3 * D, D), ((0, 32),), -0.2, 0.2)), 106.496, 434.176),
        "out_weight": normal_values(seeds[6], (D, D), (D // 2) ** -0.5, 0.3125, ((0, 32),), jnp.float32),
        "out_moment": normal_values(seeds[7], (D, D), (0.04 * TOKENS ** 0.5), 20.0, ((0, 32),), jnp.float32),
        "out_square": jnp.clip(jnp.exp(math.log(409.6) - 1.609438 * jax.random.uniform(seeds[8], (D, D), jnp.float32) ** block_scale(seeds[8], (D, D), ((0, 32),), -0.2, 0.2)), 81.92, 409.6),
        "fc_weight": normal_values(seeds[9], (FF, D), D ** -0.5, 0.21875, ((0, 32),), jnp.float32),
        "fc_moment": normal_values(seeds[10], (FF, D), (0.033 * TOKENS ** 0.5), 16.0, ((0, 32),), jnp.float32),
        "fc_square": jnp.clip(jnp.exp(math.log(155.648) - 1.3968765 * jax.random.uniform(seeds[11], (FF, D), jnp.float32) ** block_scale(seeds[11], (FF, D), ((0, 32),), -0.2, 0.2)), 38.5024, 155.648),
        "proj_weight": normal_values(seeds[12], (FF, D), FF ** -0.5, 0.109375, ((0, 32),), jnp.float32),
        "proj_moment": normal_values(seeds[13], (FF, D), (0.066 * TOKENS ** 0.5), 32.0, ((0, 32),), jnp.float32),
        "proj_square": jnp.clip(jnp.exp(math.log(622.592) - 1.3862944 * jax.random.uniform(seeds[14], (FF, D), jnp.float32) ** block_scale(seeds[14], (FF, D), ((0, 32),), -0.2, 0.2)), 155.648, 622.592),
        "vectors": draw_vectors(jax.random.fold_in(seeds[18], 71), 0),
        "vectors_moment": normal_values(seeds[16], (12, D), (0.11 * TOKENS ** 0.5), 64.0, ((1, 32),), jnp.float32),
        "vectors_square": jnp.clip(jnp.exp(math.log(1720.32) - 1.3768156 * jax.random.uniform(seeds[17], (12, D), jnp.float32) ** block_scale(seeds[17], (12, D), ((1, 32),), -0.2, 0.2)), 434.176, 1720.32),
    }


@jax.custom_vjp
def low(v):
    return lax.optimization_barrier(v.astype(jnp.bfloat16)).astype(jnp.float32)

@jax.custom_vjp
def low_back(v):
    return v

def low_keep(v):
    return (low(v), None)

def low_pass(kept, grad):
    return (grad,)

def back_keep(v):
    return (v, None)

def back_low(kept, grad):
    return (low(grad),)
low.defvjp(low_keep, low_pass)
low_back.defvjp(back_keep, back_low)
norm_eps = 1e-05
beta_one = 0.9
beta_two = 0.95
adam_eps = 1e-08
rate_matrix = 0.1
rate_vector = 0.6
decay_matrix = 0.1
score_scale = 0.125
masked_score = -1e+30
highest = lax.Precision.HIGHEST

def norm_layer(values, norm_gain, norm_bias):
    center = values - lax.optimization_barrier(jnp.mean(values, axis=-1, keepdims=True))
    spread = lax.optimization_barrier(jnp.mean(center * center, axis=-1, keepdims=True))
    return center * lax.rsqrt(spread + norm_eps) * norm_gain + norm_bias

def natural_positions(row_index):
    device = row_index // SEQ_DEV
    within = row_index % SEQ_DEV
    half_rows = SEQ_DEV // 2
    block_id = jnp.where(within < half_rows, device, 2 * N_CTX - 1 - device)
    return (block_id * half_rows + within % half_rows).astype(jnp.int32)

def document_ids(positions, seq_lengths):
    bounds = jnp.cumsum(seq_lengths)[:-1]
    return lax.optimization_barrier(jnp.sum((positions[:, None] >= bounds[None, :]).astype(jnp.int32), axis=1))

def attend(queries, key_rows, value_rows, positions, documents):
    block_rows = math.gcd(LEN, 512)
    block_count = LEN // block_rows

    def one_block(pieces):
        query_block, query_pos, query_doc = pieces
        scores = jnp.einsum('qhd,khd->hqk', query_block, key_rows, precision=highest) * score_scale
        scores = low_back(scores)
        allowed = (positions[None, :] <= query_pos[:, None]) & (documents[None, :] == query_doc[:, None])
        scores = jnp.where(allowed[None], scores, masked_score)
        row_max = lax.optimization_barrier(jnp.max(scores, axis=-1, keepdims=True))
        weights = jnp.exp(scores - row_max)
        shares = weights / lax.optimization_barrier(jnp.sum(weights, axis=-1, keepdims=True))
        return jnp.einsum('hqk,khd->qhd', low(shares), value_rows, precision=highest)
    pieces = (queries.reshape(block_count, block_rows, H, HD), positions.reshape(block_count, block_rows), documents.reshape(block_count, block_rows))
    result = lax.map(jax.checkpoint(one_block), pieces)
    return result.reshape(LEN, H * HD)

def layer(params, tokens, seq_lengths):
    qkv_low, out_low, fc_low, proj_low, vector_low = [low(master) for master in params]
    positions = natural_positions(jnp.arange(LEN, dtype=jnp.int32))
    documents = document_ids(positions, seq_lengths)
    hidden_one = low(norm_layer(tokens, vector_low[0], vector_low[1]))
    bias_qkv = jnp.concatenate([vector_low[2], jnp.zeros((D,), jnp.float32), vector_low[3]])
    mixed = jnp.dot(hidden_one, qkv_low.T, precision=highest, preferred_element_type=jnp.float32) + bias_qkv
    mixed = low(low_back(mixed))
    queries = mixed[:, :D].reshape(LEN, H, HD)
    key_rows = mixed[:, D:2 * D].reshape(LEN, H, HD)
    value_rows = mixed[:, 2 * D:].reshape(LEN, H, HD)
    attended = low(low_back(attend(queries, key_rows, value_rows, positions, documents)))
    branch = low_back(jnp.dot(attended, out_low, precision=highest, preferred_element_type=jnp.float32))
    middle = tokens + branch + vector_low[4]
    hidden_two = low(norm_layer(middle, vector_low[5], vector_low[6]))
    before = jnp.dot(hidden_two, fc_low.T, precision=highest, preferred_element_type=jnp.float32) + vector_low[8:].reshape(FF)
    before = low_back(before)
    active = low(jax.nn.gelu(before, approximate=True))
    return middle + jnp.dot(active, proj_low, precision=highest, preferred_element_type=jnp.float32) + vector_low[7]

def adam_update(weight, moment, square, gradient, rate, decay):
    moment_new = beta_one * moment + (1.0 - beta_one) * gradient
    square_new = beta_two * square + (1.0 - beta_two) * gradient * gradient
    corrected = moment_new / (1.0 - beta_one ** STEP)
    scaled = square_new / (1.0 - beta_two ** STEP)
    weight_new = weight - rate * (corrected / (jnp.sqrt(scaled) + adam_eps) + decay * weight)
    return (moment_new, square_new, weight_new)

def reference(inputs, cotangent, lengths, qkv_weight, qkv_moment, qkv_square, out_weight, out_moment, out_square, fc_weight, fc_moment, fc_square, proj_weight, proj_moment, proj_square, vectors, vectors_moment, vectors_square):
    params = (qkv_weight, out_weight, fc_weight, proj_weight, vectors)
    zeros = tuple((jnp.zeros_like(master) for master in params))

    def one_sequence(totals, pieces):
        seq_tokens, seq_cot, seq_lengths = pieces

        def forward(weights, tokens):
            return layer(weights, tokens, seq_lengths)
        output, pullback = jax.vjp(forward, params, seq_tokens.astype(jnp.float32))
        grads_now, token_grad = pullback(seq_cot.astype(jnp.float32))
        totals = tuple((running + added for running, added in zip(totals, grads_now)))
        return (totals, (output.astype(jnp.bfloat16), token_grad.astype(jnp.bfloat16)))
    totals, (layer_out, input_grad) = lax.scan(one_sequence, zeros, (inputs, cotangent, lengths))
    qkv_grad, out_grad, fc_grad, proj_grad, vectors_grad = totals
    qkv_moment_new, qkv_square_new, qkv_weight_new = adam_update(qkv_weight, qkv_moment, qkv_square, qkv_grad, rate_matrix, decay_matrix)
    out_moment_new, out_square_new, out_weight_new = adam_update(out_weight, out_moment, out_square, out_grad, rate_matrix, decay_matrix)
    fc_moment_new, fc_square_new, fc_weight_new = adam_update(fc_weight, fc_moment, fc_square, fc_grad, rate_matrix, decay_matrix)
    proj_moment_new, proj_square_new, proj_weight_new = adam_update(proj_weight, proj_moment, proj_square, proj_grad, rate_matrix, decay_matrix)
    vectors_moment_new, vectors_square_new, vectors_new = adam_update(vectors, vectors_moment, vectors_square, vectors_grad, rate_vector, 0.0)
    return (layer_out, input_grad, qkv_grad, qkv_moment_new, qkv_square_new, qkv_weight_new, out_grad, out_moment_new, out_square_new, out_weight_new, fc_grad, fc_moment_new, fc_square_new, fc_weight_new, proj_grad, proj_moment_new, proj_square_new, proj_weight_new, vectors_grad, vectors_moment_new, vectors_square_new, vectors_new)
```

```python
import functools

import jax
import jax.numpy as jnp
from jax import lax
from jax.experimental import pallas as pl
from jax.experimental.pallas import tpu as pltpu
from jax.sharding import PartitionSpec as P

H = 12
HD = 64
STEP = 10


norm_eps = 1e-05
beta_one = 0.9
beta_two = 0.95
adam_eps = 1e-08
rate_matrix = 0.1
rate_vector = 0.6
decay_matrix = 0.1
score_scale = 0.125
masked_score = -1e30


def norm_layer(values, norm_gain, norm_bias):
    center = values - jnp.mean(values, axis=-1, keepdims=True)
    spread = jnp.mean(center * center, axis=-1, keepdims=True)
    return center * lax.rsqrt(spread + norm_eps) * norm_gain + norm_bias


def gelu_tanh(values):
    return jax.nn.gelu(values, approximate=True)


def natural_positions(row_index, seq_rows, ctx_count):
    device = row_index // seq_rows
    within = row_index % seq_rows
    half_rows = seq_rows // 2
    block_id = jnp.where(within < half_rows, device, 2 * ctx_count - 1 - device)
    return block_id * half_rows + within % half_rows


def dot_rows(left, right):
    return lax.dot_general(
        left, right, (((1,), (1,)), ((), ())), preferred_element_type=jnp.float32
    )


def dot_cols(left, right):
    return lax.dot_general(
        left, right, (((0,), (0,)), ((), ())), preferred_element_type=jnp.float32
    )


def adam_update(weight, moment, square, gradient, rate, decay):
    moment_new = beta_one * moment + (1.0 - beta_one) * gradient
    square_new = beta_two * square + (1.0 - beta_two) * gradient * gradient
    corrected = moment_new / (1.0 - beta_one**STEP)
    scaled = square_new / (1.0 - beta_two**STEP)
    weight_new = weight - rate * (corrected / (jnp.sqrt(scaled) + adam_eps) + decay * weight)
    return (moment_new, square_new, weight_new)


def attention_forward_kernel(pairs, query_ref, whole_ref, low_ref, qpos_ref, kpos_ref, out_ref, exact_ref, lse_ref):
    width = pairs * HD
    key_pos = kpos_ref[...]
    query_pos = qpos_ref[...]
    causal = key_pos <= query_pos
    for pair in range(pairs):
        lanes = slice(pair * HD, (pair + 1) * HD)
        queries = query_ref[:, pair * HD : (pair + 1) * HD]
        keys = whole_ref[:, width + pair * HD : width + (pair + 1) * HD]
        values = whole_ref[:, 2 * width + pair * HD : 2 * width + (pair + 1) * HD]
        allowed = causal & (key_pos >= low_ref[:, pair : pair + 1])
        scores = jnp.where(allowed, dot_rows(queries, keys) * score_scale, masked_score)
        top = jnp.max(scores, axis=1, keepdims=True)
        weights = jnp.exp(scores - top)
        total = jnp.sum(weights, axis=1, keepdims=True)
        shares = (weights * (1.0 / total)).astype(jnp.bfloat16)
        attended = jnp.dot(shares, values, preferred_element_type=jnp.float32)
        exact_ref[:, lanes] = attended
        out_ref[:, lanes] = attended.astype(jnp.bfloat16)
        lse_ref[:, pair : pair + 1] = top + jnp.log(total)


def attention_backward_kernel(
    pairs, steps, query_ref, whole_ref, low_ref, qpos_ref, kpos_ref, exact_ref, lse_ref, grad_ref,
    out_ref, key_acc, value_acc,
):
    width = pairs * HD
    step = pl.program_id(0)
    rows = query_ref.shape[0]
    key_pos = kpos_ref[...]
    query_pos = qpos_ref[...]
    causal = key_pos <= query_pos

    @pl.when(step == 0)
    def _():
        key_acc[...] = jnp.zeros_like(key_acc)
        value_acc[...] = jnp.zeros_like(value_acc)

    here = pl.ds(pl.multiple_of(step * rows, rows), rows)
    for pair in range(pairs):
        lanes = slice(pair * HD, (pair + 1) * HD)
        queries = query_ref[:, lanes]
        keys = whole_ref[:, width + pair * HD : width + (pair + 1) * HD]
        values = whole_ref[:, 2 * width + pair * HD : 2 * width + (pair + 1) * HD]
        grads = grad_ref[:, lanes]
        allowed = causal & (key_pos >= low_ref[:, pair : pair + 1])
        scores = dot_rows(queries, keys) * score_scale
        shares = jnp.where(allowed, jnp.exp(scores - lse_ref[:, pair : pair + 1]), 0.0)
        delta = jnp.sum(grads.astype(jnp.float32) * exact_ref[:, lanes], axis=1, keepdims=True)
        grad_scores = (shares * (dot_rows(grads, values) - delta)).astype(jnp.bfloat16)
        out_ref[here, lanes] = (
            score_scale * jnp.dot(grad_scores, keys, preferred_element_type=jnp.float32)
        ).astype(jnp.bfloat16)
        key_acc[:, lanes] += dot_cols(grad_scores, queries)
        value_acc[:, lanes] += dot_cols(shares.astype(jnp.bfloat16), grads)

    @pl.when(step == steps - 1)
    def _():
        out_ref[:, width : 2 * width] = (score_scale * key_acc[...]).astype(jnp.bfloat16)
        out_ref[:, 2 * width :] = value_acc[...].astype(jnp.bfloat16)


def query_block(length):
    return 256 if length <= 1024 else 64


def attention_specs(length, pairs, block):
    return [
        pl.BlockSpec((block, 3 * pairs * HD), lambda i: (i, 0)),
        pl.BlockSpec((length, 3 * pairs * HD), lambda i: (0, 0)),
        pl.BlockSpec((block, pairs), lambda i: (i, 0)),
        pl.BlockSpec((block, 1), lambda i: (i, 0)),
        pl.BlockSpec((1, length), lambda i: (0, 0)),
    ]


def attention_forward(mixed, low, qpos, kpos):
    length, pairs = low.shape
    block = query_block(length)
    width = pairs * HD
    return pl.pallas_call(
        functools.partial(attention_forward_kernel, pairs),
        grid=(length // block,),
        in_specs=attention_specs(length, pairs, block),
        out_specs=[
            pl.BlockSpec((block, width), lambda i: (i, 0)),
            pl.BlockSpec((block, width), lambda i: (i, 0)),
            pl.BlockSpec((block, pairs), lambda i: (i, 0)),
        ],
        out_shape=[
            jax.ShapeDtypeStruct((length, width), jnp.bfloat16),
            jax.ShapeDtypeStruct((length, width), jnp.float32),
            jax.ShapeDtypeStruct((length, pairs), jnp.float32),
        ],
        compiler_params=pltpu.CompilerParams(vmem_limit_bytes=48 * 2**20),
        name="attention_forward",
    )(mixed, mixed, low, qpos, kpos)


def attention_backward(mixed, low, qpos, kpos, exact, lse, grads):
    length, pairs = low.shape
    block = query_block(length)
    width = pairs * HD
    return pl.pallas_call(
        functools.partial(attention_backward_kernel, pairs, length // block),
        grid=(length // block,),
        in_specs=attention_specs(length, pairs, block)
        + [
            pl.BlockSpec((block, width), lambda i: (i, 0)),
            pl.BlockSpec((block, pairs), lambda i: (i, 0)),
            pl.BlockSpec((block, width), lambda i: (i, 0)),
        ],
        out_specs=pl.BlockSpec((length, 3 * width), lambda i: (0, 0)),
        out_shape=jax.ShapeDtypeStruct((length, 3 * width), jnp.bfloat16),
        scratch_shapes=[
            pltpu.VMEM((length, width), jnp.float32),
            pltpu.VMEM((length, width), jnp.float32),
        ],
        compiler_params=pltpu.CompilerParams(vmem_limit_bytes=48 * 2**20),
        name="attention_backward",
    )(mixed, mixed, low, qpos, kpos, exact, lse, grads)


def tokens_to_heads(array, parts, count, pairs):
    groups, rows, width = array.shape
    array = array.reshape(groups, rows, parts, H, HD).transpose(0, 3, 1, 2, 4)
    array = array.reshape(groups * H, rows, parts, HD)
    spare = count * pairs - groups * H
    if spare:
        array = jnp.pad(array, ((0, spare), (0, 0), (0, 0), (0, 0)))
    array = array.reshape(count, pairs, rows, parts, HD).transpose(0, 2, 3, 1, 4)
    array = array.reshape(count, rows, parts * pairs * HD)
    array = lax.all_to_all(array, "ctx", 0, 0)
    return array.reshape(count * rows, parts * pairs * HD)


def heads_to_tokens(array, parts, count, pairs, groups):
    rows = array.shape[0] // count
    array = lax.all_to_all(array.reshape(count, rows, parts * pairs * HD), "ctx", 0, 0)
    array = array.reshape(count, rows, parts, pairs, HD).transpose(0, 3, 1, 2, 4)
    array = array.reshape(count * pairs, rows, parts, HD)[: groups * H]
    array = array.reshape(groups, H, rows, parts, HD).transpose(0, 2, 3, 1, 4)
    return array.reshape(groups * rows, parts * H * HD)


def local(
    inputs,
    cotangent,
    lengths,
    qkv_weight,
    qkv_moment,
    qkv_square,
    out_weight,
    out_moment,
    out_square,
    fc_weight,
    fc_moment,
    fc_square,
    proj_weight,
    proj_moment,
    proj_square,
    vectors,
    vectors_moment,
    vectors_square,
):
    groups, rows_seq, model_width = inputs.shape
    total_rows = groups * rows_seq
    ctx_count = lax.axis_size("ctx")
    device_count = ctx_count * lax.axis_size("batch")
    both = ("batch", "ctx")
    length = rows_seq * ctx_count
    pairs = -(-(groups * H) // ctx_count)

    positions = natural_positions(jnp.arange(length, dtype=jnp.int32), rows_seq, ctx_count)
    ends = jnp.cumsum(lengths, axis=1)[:, :-1]
    starts = jnp.max(
        jnp.where(positions[None, :, None] >= ends[:, None, :], ends[:, None, :], 0), axis=2
    )
    pair_seq = jnp.minimum((lax.axis_index("ctx") * pairs + jnp.arange(pairs)) // H, groups - 1)
    chosen = (pair_seq[:, None] == jnp.arange(groups)[None, :]).astype(jnp.int32)
    low = jnp.sum(starts.T[:, None, :] * chosen[None, :, :], axis=2)
    qpos, kpos = positions[:, None], positions[None, :]

    qkv_rows, out_rows = qkv_weight.shape[0], out_weight.shape[0]
    vector_cols = vectors.shape[1]
    vector_entries = vectors.size
    weight_rows = qkv_rows + out_rows
    shard_rows = -(-(weight_rows + -(-vector_entries // model_width)) // 16) * 16
    vector_tail = (shard_rows - weight_rows) * model_width - vector_entries
    vector_line = jnp.pad(vectors.reshape(-1), (0, vector_tail)).reshape(-1, model_width)
    first_shard = jnp.concatenate([qkv_weight, out_weight, vector_line], axis=0).astype(jnp.bfloat16)
    first_full = lax.all_gather(first_shard, both, axis=0, tiled=False)
    fc_full = lax.all_gather(fc_weight.astype(jnp.bfloat16), both, axis=0, tiled=True)
    proj_full = lax.all_gather(proj_weight.astype(jnp.bfloat16), both, axis=0, tiled=True)
    qkv_full = first_full[:, :qkv_rows].reshape(-1, model_width)
    out_full = first_full[:, qkv_rows : qkv_rows + out_rows].reshape(-1, model_width)
    vector_rows = (
        first_full[:, qkv_rows + out_rows :]
        .reshape(device_count, -1)[:, :vector_entries]
        .reshape(device_count, vectors.shape[0], vector_cols)
        .transpose(1, 0, 2)
        .reshape(vectors.shape[0], model_width)
        .astype(jnp.float32)
    )
    tokens = inputs.reshape(total_rows, model_width).astype(jnp.float32)
    hidden_one_low = norm_layer(tokens, vector_rows[0], vector_rows[1]).astype(jnp.bfloat16)
    bias_qkv = jnp.concatenate(
        [vector_rows[2], jnp.zeros((model_width,), jnp.float32), vector_rows[3]]
    )
    mixed_low = (dot_rows(hidden_one_low, qkv_full) + bias_qkv).astype(jnp.bfloat16)
    mixed_heads = tokens_to_heads(
        mixed_low.reshape(groups, rows_seq, 3 * model_width), 3, ctx_count, pairs
    )
    attended_heads, exact_heads, lse = attention_forward(mixed_heads, low, qpos, kpos)
    attended_low = heads_to_tokens(attended_heads, 1, ctx_count, pairs, groups)
    middle = (
        tokens
        + jnp.dot(attended_low, out_full, preferred_element_type=jnp.float32)
        + vector_rows[4]
    )
    hidden_two_low = norm_layer(middle, vector_rows[5], vector_rows[6]).astype(jnp.bfloat16)
    bias_fc = vector_rows[8:].reshape(-1)
    before = dot_rows(hidden_two_low, fc_full) + bias_fc
    active_low = gelu_tanh(before).astype(jnp.bfloat16)
    mlp_out = jnp.dot(active_low, proj_full, preferred_element_type=jnp.float32)
    layer_out = (
        (middle + mlp_out + vector_rows[7])
        .astype(jnp.bfloat16)
        .reshape(groups, rows_seq, model_width)
    )
    grad_top = cotangent.reshape(total_rows, model_width)
    grad_top_f = grad_top.astype(jnp.float32)
    proj_grad = lax.psum_scatter(
        dot_cols(active_low, grad_top).astype(jnp.bfloat16), both, scatter_dimension=0, tiled=True
    ).astype(jnp.float32)
    grad_active = dot_rows(grad_top, proj_full)
    unused, pullback = jax.vjp(gelu_tanh, before)
    grad_before = pullback(grad_active)[0].astype(jnp.bfloat16)
    fc_grad = lax.psum_scatter(
        dot_cols(grad_before, hidden_two_low).astype(jnp.bfloat16),
        both,
        scatter_dimension=0,
        tiled=True,
    ).astype(jnp.float32)
    grad_hidden_two = jnp.dot(grad_before, fc_full, preferred_element_type=jnp.float32)
    unused, pull_two = jax.vjp(norm_layer, middle, vector_rows[5], vector_rows[6])
    grad_middle_norm, grad_gain_two, grad_bias_two = pull_two(grad_hidden_two)
    grad_middle = grad_top_f + grad_middle_norm
    grad_middle_low = grad_middle.astype(jnp.bfloat16)
    out_term = dot_cols(attended_low, grad_middle_low)
    grad_attended = dot_rows(grad_middle_low, out_full).astype(jnp.bfloat16)
    grad_heads = tokens_to_heads(
        grad_attended.reshape(groups, rows_seq, model_width), 1, ctx_count, pairs
    )
    mixed_grad_heads = attention_backward(
        mixed_heads, low, qpos, kpos, exact_heads, lse, grad_heads
    )
    grad_mixed = heads_to_tokens(mixed_grad_heads, 3, ctx_count, pairs, groups)
    qkv_term = dot_cols(grad_mixed, hidden_one_low)
    grad_hidden_one = jnp.dot(grad_mixed, qkv_full, preferred_element_type=jnp.float32)
    unused, pull_one = jax.vjp(norm_layer, tokens, vector_rows[0], vector_rows[1])
    grad_tokens_norm, grad_gain_one, grad_bias_one = pull_one(grad_hidden_one)
    input_grad = (
        (grad_middle + grad_tokens_norm).astype(jnp.bfloat16).reshape(groups, rows_seq, model_width)
    )
    mixed_sums = jnp.sum(grad_mixed.astype(jnp.float32), axis=0)
    fc_sums = jnp.sum(grad_before.astype(jnp.float32), axis=0)
    vector_local = jnp.concatenate(
        [
            jnp.stack(
                [
                    grad_gain_one,
                    grad_bias_one,
                    mixed_sums[:model_width],
                    mixed_sums[2 * model_width :],
                    jnp.sum(grad_middle, axis=0),
                    grad_gain_two,
                    grad_bias_two,
                    jnp.sum(grad_top_f, axis=0),
                ]
            ),
            fc_sums.reshape(-1, model_width),
        ],
        axis=0,
    )
    vector_term = jnp.pad(
        vector_local.reshape(-1, device_count, vector_cols)
        .transpose(1, 0, 2)
        .reshape(device_count, vector_entries),
        ((0, 0), (0, vector_tail)),
    ).reshape(device_count, -1, model_width)
    last_term = jnp.concatenate(
        [
            qkv_term.astype(jnp.bfloat16).reshape(device_count, qkv_rows, model_width),
            out_term.astype(jnp.bfloat16).reshape(device_count, out_rows, model_width),
            vector_term.astype(jnp.bfloat16),
        ],
        axis=1,
    )
    last_sum = lax.psum_scatter(
        last_term.reshape(-1, model_width), both, scatter_dimension=0, tiled=True
    ).astype(jnp.float32)
    qkv_grad = last_sum[:qkv_rows]
    out_grad = last_sum[qkv_rows : qkv_rows + out_rows]
    vectors_grad = last_sum[qkv_rows + out_rows :].reshape(-1)[:vector_entries].reshape(vectors.shape)
    qkv_moment_new, qkv_square_new, qkv_weight_new = adam_update(
        qkv_weight, qkv_moment, qkv_square, qkv_grad, rate_matrix, decay_matrix
    )
    out_moment_new, out_square_new, out_weight_new = adam_update(
        out_weight, out_moment, out_square, out_grad, rate_matrix, decay_matrix
    )
    fc_moment_new, fc_square_new, fc_weight_new = adam_update(
        fc_weight, fc_moment, fc_square, fc_grad, rate_matrix, decay_matrix
    )
    proj_moment_new, proj_square_new, proj_weight_new = adam_update(
        proj_weight, proj_moment, proj_square, proj_grad, rate_matrix, decay_matrix
    )
    vectors_moment_new, vectors_square_new, vectors_new = adam_update(
        vectors, vectors_moment, vectors_square, vectors_grad, rate_vector, 0.0
    )
    return (
        layer_out,
        input_grad,
        qkv_grad,
        qkv_moment_new,
        qkv_square_new,
        qkv_weight_new,
        out_grad,
        out_moment_new,
        out_square_new,
        out_weight_new,
        fc_grad,
        fc_moment_new,
        fc_square_new,
        fc_weight_new,
        proj_grad,
        proj_moment_new,
        proj_square_new,
        proj_weight_new,
        vectors_grad,
        vectors_moment_new,
        vectors_square_new,
        vectors_new,
    )


def solution(mesh):
    in_specs = (
        P("batch", "ctx", None),
        P("batch", "ctx", None),
        P("batch", None),
        P(("batch", "ctx"), None),
        P(("batch", "ctx"), None),
        P(("batch", "ctx"), None),
        P(("batch", "ctx"), None),
        P(("batch", "ctx"), None),
        P(("batch", "ctx"), None),
        P(("batch", "ctx"), None),
        P(("batch", "ctx"), None),
        P(("batch", "ctx"), None),
        P(("batch", "ctx"), None),
        P(("batch", "ctx"), None),
        P(("batch", "ctx"), None),
        P(None, ("batch", "ctx")),
        P(None, ("batch", "ctx")),
        P(None, ("batch", "ctx")),
    )
    out_specs = (
        P("batch", "ctx", None),
        P("batch", "ctx", None),
        P(("batch", "ctx"), None),
        P(("batch", "ctx"), None),
        P(("batch", "ctx"), None),
        P(("batch", "ctx"), None),
        P(("batch", "ctx"), None),
        P(("batch", "ctx"), None),
        P(("batch", "ctx"), None),
        P(("batch", "ctx"), None),
        P(("batch", "ctx"), None),
        P(("batch", "ctx"), None),
        P(("batch", "ctx"), None),
        P(("batch", "ctx"), None),
        P(("batch", "ctx"), None),
        P(("batch", "ctx"), None),
        P(("batch", "ctx"), None),
        P(("batch", "ctx"), None),
        P(None, ("batch", "ctx")),
        P(None, ("batch", "ctx")),
        P(None, ("batch", "ctx")),
        P(None, ("batch", "ctx")),
    )
    return jax.shard_map(local, mesh=mesh, in_specs=in_specs, out_specs=out_specs, check_vma=False)
```

```python
import functools

import jax
import jax.numpy as jnp
from jax import lax
from jax.experimental import pallas as pl
from jax.experimental.pallas import tpu as pltpu
from jax.sharding import PartitionSpec as P

H = 12
HD = 64
STEP = 10


norm_eps = 1e-05
beta_one = 0.9
beta_two = 0.95
adam_eps = 1e-08
rate_matrix = 0.1
rate_vector = 0.6
decay_matrix = 0.1
score_scale = 0.125
masked_score = -1e30


def norm_layer(values, norm_gain, norm_bias):
    center = values - jnp.mean(values, axis=-1, keepdims=True)
    spread = jnp.mean(center * center, axis=-1, keepdims=True)
    return center * lax.rsqrt(spread + norm_eps) * norm_gain + norm_bias


def gelu_tanh(values):
    return jax.nn.gelu(values, approximate=True)


def natural_positions(row_index, seq_rows, ctx_count):
    device = row_index // seq_rows
    within = row_index % seq_rows
    half_rows = seq_rows // 2
    block_id = jnp.where(within < half_rows, device, 2 * ctx_count - 1 - device)
    return block_id * half_rows + within % half_rows


def dot_rows(left, right):
    return lax.dot_general(
        left, right, (((1,), (1,)), ((), ())), preferred_element_type=jnp.float32
    )


def dot_cols(left, right):
    return lax.dot_general(
        left, right, (((0,), (0,)), ((), ())), preferred_element_type=jnp.float32
    )


def adam_update(weight, moment, square, gradient, rate, decay):
    moment_new = beta_one * moment + (1.0 - beta_one) * gradient
    square_new = beta_two * square + (1.0 - beta_two) * gradient * gradient
    corrected = moment_new / (1.0 - beta_one**STEP)
    scaled = square_new / (1.0 - beta_two**STEP)
    weight_new = weight - rate * (corrected / (jnp.sqrt(scaled) + adam_eps) + decay * weight)
    return (moment_new, square_new, weight_new)


def attention_forward_kernel(pairs, query_ref, whole_ref, low_ref, qpos_ref, kpos_ref, out_ref, exact_ref, lse_ref):
    width = pairs * HD
    key_pos = kpos_ref[...]
    query_pos = qpos_ref[...]
    causal = key_pos <= query_pos
    for pair in range(pairs):
        lanes = slice(pair * HD, (pair + 1) * HD)
        queries = query_ref[:, pair * HD : (pair + 1) * HD]
        keys = whole_ref[:, width + pair * HD : width + (pair + 1) * HD]
        values = whole_ref[:, 2 * width + pair * HD : 2 * width + (pair + 1) * HD]
        allowed = causal & (key_pos >= low_ref[:, pair : pair + 1])
        scores = jnp.where(allowed, dot_rows(queries, keys) * score_scale, masked_score)
        top = jnp.max(scores, axis=1, keepdims=True)
        weights = jnp.exp(scores - top)
        total = jnp.sum(weights, axis=1, keepdims=True)
        shares = (weights * (1.0 / total)).astype(jnp.bfloat16)
        attended = jnp.dot(shares, values, preferred_element_type=jnp.float32)
        exact_ref[:, lanes] = attended
        out_ref[:, lanes] = attended.astype(jnp.bfloat16)
        lse_ref[:, pair : pair + 1] = top + jnp.log(total)


def attention_backward_kernel(
    pairs, steps, query_ref, whole_ref, low_ref, qpos_ref, kpos_ref, exact_ref, lse_ref, grad_ref,
    out_ref, key_acc, value_acc,
):
    width = pairs * HD
    step = pl.program_id(0)
    rows = query_ref.shape[0]
    key_pos = kpos_ref[...]
    query_pos = qpos_ref[...]
    causal = key_pos <= query_pos

    @pl.when(step == 0)
    def _():
        key_acc[...] = jnp.zeros_like(key_acc)
        value_acc[...] = jnp.zeros_like(value_acc)

    here = pl.ds(pl.multiple_of(step * rows, rows), rows)
    for pair in range(pairs):
        lanes = slice(pair * HD, (pair + 1) * HD)
        queries = query_ref[:, lanes]
        keys = whole_ref[:, width + pair * HD : width + (pair + 1) * HD]
        values = whole_ref[:, 2 * width + pair * HD : 2 * width + (pair + 1) * HD]
        grads = grad_ref[:, lanes]
        allowed = causal & (key_pos >= low_ref[:, pair : pair + 1])
        scores = dot_rows(queries, keys) * score_scale
        shares = jnp.where(allowed, jnp.exp(scores - lse_ref[:, pair : pair + 1]), 0.0)
        delta = jnp.sum(grads.astype(jnp.float32) * exact_ref[:, lanes], axis=1, keepdims=True)
        grad_scores = (shares * (dot_rows(grads, values) - delta)).astype(jnp.bfloat16)
        out_ref[here, lanes] = (
            score_scale * jnp.dot(grad_scores, keys, preferred_element_type=jnp.float32)
        ).astype(jnp.bfloat16)
        key_acc[:, lanes] += dot_cols(grad_scores, queries)
        value_acc[:, lanes] += dot_cols(shares.astype(jnp.bfloat16), grads)

    @pl.when(step == steps - 1)
    def _():
        out_ref[:, width : 2 * width] = (score_scale * key_acc[...]).astype(jnp.bfloat16)
        out_ref[:, 2 * width :] = value_acc[...].astype(jnp.bfloat16)


def query_block(length):
    return 256 if length <= 1024 else 64


def attention_specs(length, pairs, block):
    return [
        pl.BlockSpec((block, 3 * pairs * HD), lambda i: (i, 0)),
        pl.BlockSpec((length, 3 * pairs * HD), lambda i: (0, 0)),
        pl.BlockSpec((block, pairs), lambda i: (i, 0)),
        pl.BlockSpec((block, 1), lambda i: (i, 0)),
        pl.BlockSpec((1, length), lambda i: (0, 0)),
    ]


def attention_forward(mixed, low, qpos, kpos):
    length, pairs = low.shape
    block = query_block(length)
    width = pairs * HD
    return pl.pallas_call(
        functools.partial(attention_forward_kernel, pairs),
        grid=(length // block,),
        in_specs=attention_specs(length, pairs, block),
        out_specs=[
            pl.BlockSpec((block, width), lambda i: (i, 0)),
            pl.BlockSpec((block, width), lambda i: (i, 0)),
            pl.BlockSpec((block, pairs), lambda i: (i, 0)),
        ],
        out_shape=[
            jax.ShapeDtypeStruct((length, width), jnp.bfloat16),
            jax.ShapeDtypeStruct((length, width), jnp.float32),
            jax.ShapeDtypeStruct((length, pairs), jnp.float32),
        ],
        compiler_params=pltpu.CompilerParams(vmem_limit_bytes=48 * 2**20),
        name="attention_forward",
    )(mixed, mixed, low, qpos, kpos)


def attention_backward(mixed, low, qpos, kpos, exact, lse, grads):
    length, pairs = low.shape
    block = query_block(length)
    width = pairs * HD
    return pl.pallas_call(
        functools.partial(attention_backward_kernel, pairs, length // block),
        grid=(length // block,),
        in_specs=attention_specs(length, pairs, block)
        + [
            pl.BlockSpec((block, width), lambda i: (i, 0)),
            pl.BlockSpec((block, pairs), lambda i: (i, 0)),
            pl.BlockSpec((block, width), lambda i: (i, 0)),
        ],
        out_specs=pl.BlockSpec((length, 3 * width), lambda i: (0, 0)),
        out_shape=jax.ShapeDtypeStruct((length, 3 * width), jnp.bfloat16),
        scratch_shapes=[
            pltpu.VMEM((length, width), jnp.float32),
            pltpu.VMEM((length, width), jnp.float32),
        ],
        compiler_params=pltpu.CompilerParams(vmem_limit_bytes=48 * 2**20),
        name="attention_backward",
    )(mixed, mixed, low, qpos, kpos, exact, lse, grads)


def tokens_to_heads(array, parts, count, pairs):
    groups, rows, width = array.shape
    array = array.reshape(groups, rows, parts, H, HD).transpose(0, 3, 1, 2, 4)
    array = array.reshape(groups * H, rows, parts, HD)
    spare = count * pairs - groups * H
    if spare:
        array = jnp.pad(array, ((0, spare), (0, 0), (0, 0), (0, 0)))
    array = array.reshape(count, pairs, rows, parts, HD).transpose(0, 2, 3, 1, 4)
    array = array.reshape(count, rows, parts * pairs * HD)
    array = lax.all_to_all(array, "ctx", 0, 0)
    return array.reshape(count * rows, parts * pairs * HD)


def heads_to_tokens(array, parts, count, pairs, groups):
    rows = array.shape[0] // count
    array = lax.all_to_all(array.reshape(count, rows, parts * pairs * HD), "ctx", 0, 0)
    array = array.reshape(count, rows, parts, pairs, HD).transpose(0, 3, 1, 2, 4)
    array = array.reshape(count * pairs, rows, parts, HD)[: groups * H]
    array = array.reshape(groups, H, rows, parts, HD).transpose(0, 2, 3, 1, 4)
    return array.reshape(groups * rows, parts * H * HD)


grid_orders = ((4, 1, 0, 3, 2), (4, 0, 3, 2, 1), (4, 3, 2, 1, 0))


def drop_axis(index, axis, bit):
    return index[:axis] + (bit,) + index[axis:]


def scatter_sum_kernel(*refs):
    terms, sums = refs[:3], refs[3:6]
    landed = [refs[6 + 5 * part : 11 + 5 * part] for part in range(3)]
    send_sem, recv_sem = refs[21:]
    batch, ctx = lax.axis_index("batch"), lax.axis_index("ctx")
    bits = (
        lax.div(batch, 2),
        lax.rem(batch, 2),
        lax.div(ctx, 4),
        lax.rem(lax.div(ctx, 2), 2),
        lax.rem(ctx, 2),
    )
    partners = (
        (batch + 2 - 4 * bits[0], ctx),
        (batch + 1 - 2 * bits[1], ctx),
        (batch, ctx + 4 - 8 * bits[2]),
        (batch, ctx + 2 - 4 * bits[3]),
        (batch, ctx + 1 - 2 * bits[4]),
    )
    barrier = pltpu.get_barrier_semaphore()
    for partner in partners:
        pl.semaphore_signal(
            barrier, inc=1, device_id=partner, device_id_type=pl.DeviceIdType.MESH
        )
    pl.semaphore_wait(barrier, 5)

    def place(part, stage):
        axis = grid_orders[part][stage]
        return axis, sum(1 for earlier in grid_orders[part][:stage] if earlier < axis)

    def begin(part, stage):
        axis, gone = place(part, stage)
        source = terms[part] if stage == 0 else landed[part][stage - 1]
        lead = (slice(None),) * (axis - gone)
        copy = pltpu.make_async_remote_copy(
            src_ref=source.at[lead + (1 - bits[axis],)],
            dst_ref=landed[part][stage],
            send_sem=send_sem.at[part, stage],
            recv_sem=recv_sem.at[part, stage],
            device_id=partners[axis],
            device_id_type=pl.DeviceIdType.MESH,
        )
        copy.start()
        return copy

    copies = {(part, 0): begin(part, 0) for part in range(3)}
    for stage in range(5):
        for part in range(3):
            axis, gone = place(part, stage)
            source = terms[part] if stage == 0 else landed[part][stage - 1]
            target = landed[part][stage]
            copies[part, stage].wait_recv()
            left = 4 - stage
            if left:

                @pl.loop(0, 2**left)
                def _(turn):
                    index = tuple(
                        lax.rem(lax.div(turn, 2 ** (left - 1 - level)), 2) for level in range(left)
                    )
                    target[index] = target[index] + source[drop_axis(index, axis - gone, bits[axis])]

                copies[part, stage + 1] = begin(part, stage + 1)
            else:
                sums[part][...] = target[...].astype(jnp.float32) + source[bits[axis]].astype(
                    jnp.float32
                )
    for copy in copies.values():
        copy.wait_send()


def scatter_sums(terms):
    batch_count, ctx_count = lax.axis_size("batch"), lax.axis_size("ctx")
    devices = batch_count * ctx_count
    rows = [term.shape[0] // devices for term in terms]
    width = terms[0].shape[1]
    if (batch_count, ctx_count) != (4, 8) or any(count % 16 for count in rows):
        return [
            lax.psum_scatter(
                term, ("batch", "ctx"), scatter_dimension=0, tiled=True
            ).astype(jnp.float32)
            for term in terms
        ]
    whole = pl.BlockSpec(memory_space=pltpu.VMEM)
    return pl.pallas_call(
        scatter_sum_kernel,
        in_specs=[whole] * 3,
        out_specs=[whole] * 3,
        out_shape=[jax.ShapeDtypeStruct((count, width), jnp.float32) for count in rows],
        scratch_shapes=[
            pltpu.VMEM((2,) * (4 - stage) + (count, width), jnp.bfloat16)
            for count in rows
            for stage in range(5)
        ]
        + [pltpu.SemaphoreType.DMA((3, 5)), pltpu.SemaphoreType.DMA((3, 5))],
        compiler_params=pltpu.CompilerParams(
            collective_id=0, has_side_effects=True, vmem_limit_bytes=52 * 2**20
        ),
        name="scatter_sum",
    )(*[term.reshape((2,) * 5 + (count, width)) for term, count in zip(terms, rows)])


def local(
    inputs,
    cotangent,
    lengths,
    qkv_weight,
    qkv_moment,
    qkv_square,
    out_weight,
    out_moment,
    out_square,
    fc_weight,
    fc_moment,
    fc_square,
    proj_weight,
    proj_moment,
    proj_square,
    vectors,
    vectors_moment,
    vectors_square,
):
    groups, rows_seq, model_width = inputs.shape
    total_rows = groups * rows_seq
    ctx_count = lax.axis_size("ctx")
    device_count = ctx_count * lax.axis_size("batch")
    both = ("batch", "ctx")
    length = rows_seq * ctx_count
    pairs = -(-(groups * H) // ctx_count)

    positions = natural_positions(jnp.arange(length, dtype=jnp.int32), rows_seq, ctx_count)
    ends = jnp.cumsum(lengths, axis=1)[:, :-1]
    starts = jnp.max(
        jnp.where(positions[None, :, None] >= ends[:, None, :], ends[:, None, :], 0), axis=2
    )
    pair_seq = jnp.minimum((lax.axis_index("ctx") * pairs + jnp.arange(pairs)) // H, groups - 1)
    chosen = (pair_seq[:, None] == jnp.arange(groups)[None, :]).astype(jnp.int32)
    low = jnp.sum(starts.T[:, None, :] * chosen[None, :, :], axis=2)
    qpos, kpos = positions[:, None], positions[None, :]

    qkv_rows, out_rows = qkv_weight.shape[0], out_weight.shape[0]
    vector_cols = vectors.shape[1]
    vector_entries = vectors.size
    weight_rows = qkv_rows + out_rows
    shard_rows = -(-(weight_rows + -(-vector_entries // model_width)) // 16) * 16
    vector_tail = (shard_rows - weight_rows) * model_width - vector_entries
    vector_line = jnp.pad(vectors.reshape(-1), (0, vector_tail)).reshape(-1, model_width)
    first_shard = jnp.concatenate([qkv_weight, out_weight, vector_line], axis=0).astype(jnp.bfloat16)
    first_full = lax.all_gather(first_shard, both, axis=0, tiled=False)
    fc_full = lax.all_gather(fc_weight.astype(jnp.bfloat16), both, axis=0, tiled=True)
    proj_full = lax.all_gather(proj_weight.astype(jnp.bfloat16), both, axis=0, tiled=True)
    qkv_full = first_full[:, :qkv_rows].reshape(-1, model_width)
    out_full = first_full[:, qkv_rows : qkv_rows + out_rows].reshape(-1, model_width)
    vector_rows = (
        first_full[:, qkv_rows + out_rows :]
        .reshape(device_count, -1)[:, :vector_entries]
        .reshape(device_count, vectors.shape[0], vector_cols)
        .transpose(1, 0, 2)
        .reshape(vectors.shape[0], model_width)
        .astype(jnp.float32)
    )
    tokens = inputs.reshape(total_rows, model_width).astype(jnp.float32)
    hidden_one_low = norm_layer(tokens, vector_rows[0], vector_rows[1]).astype(jnp.bfloat16)
    bias_qkv = jnp.concatenate(
        [vector_rows[2], jnp.zeros((model_width,), jnp.float32), vector_rows[3]]
    )
    mixed_low = (dot_rows(hidden_one_low, qkv_full) + bias_qkv).astype(jnp.bfloat16)
    mixed_heads = tokens_to_heads(
        mixed_low.reshape(groups, rows_seq, 3 * model_width), 3, ctx_count, pairs
    )
    attended_heads, exact_heads, lse = attention_forward(mixed_heads, low, qpos, kpos)
    attended_low = heads_to_tokens(attended_heads, 1, ctx_count, pairs, groups)
    middle = (
        tokens
        + jnp.dot(attended_low, out_full, preferred_element_type=jnp.float32)
        + vector_rows[4]
    )
    hidden_two_low = norm_layer(middle, vector_rows[5], vector_rows[6]).astype(jnp.bfloat16)
    bias_fc = vector_rows[8:].reshape(-1)
    before = dot_rows(hidden_two_low, fc_full) + bias_fc
    active_low = gelu_tanh(before).astype(jnp.bfloat16)
    mlp_out = jnp.dot(active_low, proj_full, preferred_element_type=jnp.float32)
    layer_out = (
        (middle + mlp_out + vector_rows[7])
        .astype(jnp.bfloat16)
        .reshape(groups, rows_seq, model_width)
    )
    grad_top = cotangent.reshape(total_rows, model_width)
    grad_top_f = grad_top.astype(jnp.float32)
    proj_term = dot_cols(active_low, grad_top).astype(jnp.bfloat16)
    grad_active = dot_rows(grad_top, proj_full)
    unused, pullback = jax.vjp(gelu_tanh, before)
    grad_before = pullback(grad_active)[0].astype(jnp.bfloat16)
    fc_term = dot_cols(grad_before, hidden_two_low).astype(jnp.bfloat16)
    grad_hidden_two = jnp.dot(grad_before, fc_full, preferred_element_type=jnp.float32)
    unused, pull_two = jax.vjp(norm_layer, middle, vector_rows[5], vector_rows[6])
    grad_middle_norm, grad_gain_two, grad_bias_two = pull_two(grad_hidden_two)
    grad_middle = grad_top_f + grad_middle_norm
    grad_middle_low = grad_middle.astype(jnp.bfloat16)
    out_term = dot_cols(attended_low, grad_middle_low)
    grad_attended = dot_rows(grad_middle_low, out_full).astype(jnp.bfloat16)
    grad_heads = tokens_to_heads(
        grad_attended.reshape(groups, rows_seq, model_width), 1, ctx_count, pairs
    )
    mixed_grad_heads = attention_backward(
        mixed_heads, low, qpos, kpos, exact_heads, lse, grad_heads
    )
    grad_mixed = heads_to_tokens(mixed_grad_heads, 3, ctx_count, pairs, groups)
    qkv_term = dot_cols(grad_mixed, hidden_one_low)
    grad_hidden_one = jnp.dot(grad_mixed, qkv_full, preferred_element_type=jnp.float32)
    unused, pull_one = jax.vjp(norm_layer, tokens, vector_rows[0], vector_rows[1])
    grad_tokens_norm, grad_gain_one, grad_bias_one = pull_one(grad_hidden_one)
    input_grad = (
        (grad_middle + grad_tokens_norm).astype(jnp.bfloat16).reshape(groups, rows_seq, model_width)
    )
    mixed_sums = jnp.sum(grad_mixed.astype(jnp.float32), axis=0)
    fc_sums = jnp.sum(grad_before.astype(jnp.float32), axis=0)
    vector_local = jnp.concatenate(
        [
            jnp.stack(
                [
                    grad_gain_one,
                    grad_bias_one,
                    mixed_sums[:model_width],
                    mixed_sums[2 * model_width :],
                    jnp.sum(grad_middle, axis=0),
                    grad_gain_two,
                    grad_bias_two,
                    jnp.sum(grad_top_f, axis=0),
                ]
            ),
            fc_sums.reshape(-1, model_width),
        ],
        axis=0,
    )
    vector_term = jnp.pad(
        vector_local.reshape(-1, device_count, vector_cols)
        .transpose(1, 0, 2)
        .reshape(device_count, vector_entries),
        ((0, 0), (0, vector_tail)),
    ).reshape(device_count, -1, model_width)
    last_term = jnp.concatenate(
        [
            qkv_term.astype(jnp.bfloat16).reshape(device_count, qkv_rows, model_width),
            out_term.astype(jnp.bfloat16).reshape(device_count, out_rows, model_width),
            vector_term.astype(jnp.bfloat16),
        ],
        axis=1,
    )
    last_sum, fc_grad, proj_grad = scatter_sums(
        [last_term.reshape(-1, model_width), fc_term, proj_term]
    )
    qkv_grad = last_sum[:qkv_rows]
    out_grad = last_sum[qkv_rows : qkv_rows + out_rows]
    vectors_grad = last_sum[qkv_rows + out_rows :].reshape(-1)[:vector_entries].reshape(vectors.shape)
    qkv_moment_new, qkv_square_new, qkv_weight_new = adam_update(
        qkv_weight, qkv_moment, qkv_square, qkv_grad, rate_matrix, decay_matrix
    )
    out_moment_new, out_square_new, out_weight_new = adam_update(
        out_weight, out_moment, out_square, out_grad, rate_matrix, decay_matrix
    )
    fc_moment_new, fc_square_new, fc_weight_new = adam_update(
        fc_weight, fc_moment, fc_square, fc_grad, rate_matrix, decay_matrix
    )
    proj_moment_new, proj_square_new, proj_weight_new = adam_update(
        proj_weight, proj_moment, proj_square, proj_grad, rate_matrix, decay_matrix
    )
    vectors_moment_new, vectors_square_new, vectors_new = adam_update(
        vectors, vectors_moment, vectors_square, vectors_grad, rate_vector, 0.0
    )
    return (
        layer_out,
        input_grad,
        qkv_grad,
        qkv_moment_new,
        qkv_square_new,
        qkv_weight_new,
        out_grad,
        out_moment_new,
        out_square_new,
        out_weight_new,
        fc_grad,
        fc_moment_new,
        fc_square_new,
        fc_weight_new,
        proj_grad,
        proj_moment_new,
        proj_square_new,
        proj_weight_new,
        vectors_grad,
        vectors_moment_new,
        vectors_square_new,
        vectors_new,
    )


def solution(mesh):
    in_specs = (
        P("batch", "ctx", None),
        P("batch", "ctx", None),
        P("batch", None),
        P(("batch", "ctx"), None),
        P(("batch", "ctx"), None),
        P(("batch", "ctx"), None),
        P(("batch", "ctx"), None),
        P(("batch", "ctx"), None),
        P(("batch", "ctx"), None),
        P(("batch", "ctx"), None),
        P(("batch", "ctx"), None),
        P(("batch", "ctx"), None),
        P(("batch", "ctx"), None),
        P(("batch", "ctx"), None),
        P(("batch", "ctx"), None),
        P(None, ("batch", "ctx")),
        P(None, ("batch", "ctx")),
        P(None, ("batch", "ctx")),
    )
    out_specs = (
        P("batch", "ctx", None),
        P("batch", "ctx", None),
        P(("batch", "ctx"), None),
        P(("batch", "ctx"), None),
        P(("batch", "ctx"), None),
        P(("batch", "ctx"), None),
        P(("batch", "ctx"), None),
        P(("batch", "ctx"), None),
        P(("batch", "ctx"), None),
        P(("batch", "ctx"), None),
        P(("batch", "ctx"), None),
        P(("batch", "ctx"), None),
        P(("batch", "ctx"), None),
        P(("batch", "ctx"), None),
        P(("batch", "ctx"), None),
        P(("batch", "ctx"), None),
        P(("batch", "ctx"), None),
        P(("batch", "ctx"), None),
        P(None, ("batch", "ctx")),
        P(None, ("batch", "ctx")),
        P(None, ("batch", "ctx")),
        P(None, ("batch", "ctx")),
    )
    return jax.shard_map(local, mesh=mesh, in_specs=in_specs, out_specs=out_specs, check_vma=False)
```
